32 devices in a mesh: groups: 2 (over y), row: 4 (over x, core), col: 4 (over z).
Axes of the slice: x: 2, y: 2, z: 4, core: 2. Of those that a mesh axis runs over, the one named last changes fastest.
Arguments:
- channels: bfloat16 [4, 16, 64, 8192], P('groups', None, 'row', 'col'), parts along dimension 0, may hold values from -6 to 6
- weights: float32 [32, 64], P('groups'), parts along dimension 0, may hold values from 0.25 to 4
- slab_in: float32 [2, 512, 8192], P(None, ('groups', 'row'), 'col'), parts along dimension 1, may hold values from -0.6 to 0.6
Outputs:
- slab_out: float32 [2, 512, 8192], P(None, ('groups', 'row'), 'col'), parts along dimension 1
The draws below stay inside these ranges and needn't reach their ends.
There are 2 independent parts, one for each index of `groups`. The reference program is written for one: setup_inputs(seed, part) draws one part's arguments, and reference() takes and returns one part's arrays. A program takes and returns all parts, laid end to end along the dimension named above; each array names one. Nothing has to cross between parts.
All inputs are finite; a program needn't handle non-finite values.
Results may differ from the reference program's by a relative error of at most 0.0015.
Values may be sent and summed in bfloat16 or wider, within the bound.
A program may use at most 64 MiB of HBM per device.

```python
import math
import jax
import jax.numpy as jnp
from jax import lax

S = 64
PANELS = 16
SLAB = 256
ORDER = 8192


def block_scale(key, shape, split, low, high):
    gain = 1.0
    for position, blocks in split:
        heights = jax.random.uniform(jax.random.fold_in(jax.random.fold_in(key, 6), position), (blocks,), jnp.float32, low / len(split), high / len(split))
        gain = gain * jnp.repeat(jnp.exp(heights), shape[position] // blocks).reshape((-1,) + (1,) * (len(shape) - 1 - position))
    return gain


def bell_draw(rng, dims, scale, bound, pieces=(), held_as=jnp.bfloat16):
    result = scale * jax.random.normal(rng, dims, jnp.float32)
    if pieces:
        result = result * block_scale(rng, dims, pieces, -0.22, 0.18)
    return jnp.clip(result, -bound, bound).astype(held_as)


def setup_inputs(seed: int = 0, part: int = 0) -> dict:
    splits = jax.random.split(jax.random.key(seed), 4)
    part_keys = jax.random.split(jax.random.fold_in(splits[3], part), 4)
    return {
        "channels": bell_draw(part_keys[0], (2, PANELS, S, ORDER), 1.0, 6.0, ((2, 4), (3, 4))),
        "weights": jnp.clip(jnp.exp(jax.random.uniform(part_keys[1], (PANELS, S), jnp.float32, math.log(0.25), math.log(4.0))), 0.25, 4.0),
        "slab_in": bell_draw(part_keys[2], (2, SLAB, ORDER), 0.1, 0.6, ((1, 4), (2, 4)), jnp.float32),
    }


def product(left_part, right_part):
    contract_dims = (((0, 1), (0, 1)), ((), ()))
    return lax.dot_general(left_part, right_part, contract_dims, preferred_element_type=jnp.float32)


def reference(channels, weights, slab_in):
    weight_total = jnp.sum(weights)
    scaled = (weights / weight_total)[None, :, :, None]
    slab_rows = (channels[:, :, :, :SLAB].astype(jnp.float32) * scaled).astype(jnp.bfloat16)
    real_part = product(slab_rows[0], channels[0]) + product(slab_rows[1], channels[1])
    imag_part = product(slab_rows[0], channels[1]) - product(slab_rows[1], channels[0])
    return slab_in + jnp.stack([real_part, imag_part])
```

```python
import functools

import jax
import jax.numpy as jnp
from jax import lax
from jax.experimental import pallas as pl
from jax.experimental.pallas import tpu as pltpu
from jax.sharding import PartitionSpec as P

F32, BF16 = jnp.float32, jnp.bfloat16
MESH = pl.DeviceIdType.MESH


def kernel(
    chips, cols, blocks, direct, tile,
    channels, weights, slab, out,
    right, left, split, head, turned, total, sent, got,
    own_sem, pair_send, pair_recv, head_sem, slab_sem,
    left_send, left_recv, row_send, row_recv, out_sem,
):
    row, z = lax.axis_index("row"), lax.axis_index("col")
    x, c = row // 2, lax.rem(row, 2)
    pair = row + 1 - 2 * c
    depth, width = channels.shape[1:]
    rows = slab.shape[1]
    high = rows // blocks
    panels = weights.shape[0]
    samples = depth // panels
    tiles = width // tile
    steps = list(range(1, chips)) + [0]

    def peer(d):
        return 2 * lax.rem(x + d, chips) + c

    barrier = pltpu.get_barrier_semaphore()

    def greet(to_row, to_col):
        pl.semaphore_signal(barrier, 1, device_id={"row": to_row, "col": to_col}, device_id_type=MESH)

    greet(pair, z)
    for d in range(1, chips):
        greet(peer(d), z)

    @pl.when(z > 0)
    def _():
        greet(row, 0)
        greet(pair, 0)

    @pl.when(z > 1)
    def _():
        greet(row, z - 1)

    def head_copy(d):
        start = pl.multiple_of(lax.rem(x + d, chips) * (2 * rows), 2 * rows)
        return pltpu.make_async_copy(channels.at[:, :, pl.ds(start, 2 * rows)], head.at[d], head_sem.at[d])

    def own_copy(n):
        span = pl.ds(n * tile, tile)
        return pltpu.make_async_copy(channels.at[:, :, span], right.at[c, :, :, span], own_sem.at[n])

    def pair_copy(n, side):
        span = pl.ds(n * tile, tile)
        return pltpu.make_async_remote_copy(
            channels.at[:, :, span], right.at[side, :, :, span], pair_send.at[n], pair_recv.at[n],
            device_id={"row": pair, "col": z}, device_id_type=MESH)

    def left_copy(d, b, source, side, slot, to_row, to_col):
        return pltpu.make_async_remote_copy(
            source, left.at[d, b, side], left_send.at[d, b, slot], left_recv.at[d, b, side],
            device_id={"row": to_row, "col": to_col}, device_id_type=MESH)

    def row_copy(d, b):
        return pltpu.make_async_remote_copy(
            sent.at[d - 1, b], got.at[d - 1, b], row_send.at[d - 1, b], row_recv.at[d - 1, b],
            device_id={"row": peer(d), "col": z}, device_id_type=MESH)

    def out_copy(b):
        span = pl.ds(b * high, high)
        return pltpu.make_async_copy(total.at[:, span], out.at[:, span], out_sem.at[b])

    slab_copy = pltpu.make_async_copy(slab, total, slab_sem)

    @pl.when(z == 0)
    def _():
        for d in steps:
            head_copy(d).start()

    for n in range(tiles):
        own_copy(n).start()
    slab_copy.start()

    def head_sends(d, b):
        copies = [left_copy(d, b, split.at[d, 1 - c, b], c, 0, pair, z)]
        for far in (range(cols - 1, 0, -1) if direct and d else [1] if cols > 1 else []):
            copies.append(left_copy(d, b, split.at[d, c, b], c, 2 * far - 1, row, far))
            copies.append(left_copy(d, b, split.at[d, 1 - c, b], c, 2 * far, pair, far))
        return copies

    @pl.when(z == 0)
    def _():
        scaled = weights[...] / jnp.sum(weights[...])
        turned[...] = scaled.T
        mine = turned[pl.ds(pl.multiple_of(row * samples, samples), samples), :]
        gain = jnp.concatenate([jnp.broadcast_to(mine[:, p:p + 1], (samples, 2 * rows)) for p in range(panels)])
        for d in steps:
            head_copy(d).wait()
            for part in range(2):
                value = (head[d, part].astype(F32) * gain).T.astype(BF16)
                for side in range(2):
                    for b in range(blocks):
                        split[d, side, b, part] = value[side * rows + b * high:side * rows + (b + 1) * high]
            for b in range(blocks):
                left[d, b, c] = split[d, c, b]
            if d == steps[0]:
                pl.semaphore_wait(barrier, 2 * cols - 1 + chips - 1)
            for b in range(blocks):
                for copy in head_sends(d, b):
                    copy.start()
            if d == steps[0]:
                for n in range(tiles):
                    pair_copy(n, c).start()

    @pl.when(z > 0)
    def _():
        pl.semaphore_wait(barrier, 1 + chips - 1 + jnp.where(z < cols - 1, 1, 0))
        for n in range(tiles):
            pair_copy(n, c).start()

    def forwards(d):
        return not (direct and d)

    def take_left(d, b):
        @pl.when(z == 0)
        def _():
            left_copy(d, b, left.at[d, b, 1 - c], 1 - c, 0, pair, z).wait_recv()

        @pl.when(z > 0)
        def _():
            for side in range(2):
                left_copy(d, b, left.at[d, b, side], side, side, pair, z).wait_recv()
                if forwards(d):
                    @pl.when(z < cols - 1)
                    def _():
                        left_copy(d, b, left.at[d, b, side], side, side, row, z + 1).start()

    def multiply(d, b, first):
        real, imag = [], []
        for side in range(2):
            re, im = left[d, b, side, 0], left[d, b, side, 1]
            real += [re, im]
            imag += [-im, re]
        rows_in = jnp.concatenate([jnp.concatenate(real, axis=1), jnp.concatenate(imag, axis=1)], axis=0)

        def one(n):
            span = pl.ds(pl.multiple_of(n * tile, tile), tile)
            block = right[:, :, :, span].reshape(4 * depth, tile)
            value = jnp.dot(rows_in, block, preferred_element_type=F32).reshape(2, high, tile)
            if d:
                sent[d - 1, b, :, :, span] = value.astype(BF16)
            else:
                total[:, pl.ds(b * high, high), span] += value

        if first:
            for n in range(tiles):
                own_copy(n).wait()
                pair_copy(n, 1 - c).wait_recv()
                one(n)
        else:
            pl.loop(0, tiles)(one)

    first = True
    for d in steps:
        if d == 0:
            slab_copy.wait()
        for b in range(blocks):
            take_left(d, b)
            multiply(d, b, first)
            first = False
            if d:
                row_copy(d, b).start()

    for b in range(blocks):
        span = pl.ds(b * high, high)
        for d in range(1, chips):
            row_copy(d, b).wait_recv()
            total[:, span] += got[d - 1, b].astype(F32)
        out_copy(b).start()

    for n in range(tiles):
        pair_copy(n, c).wait_send()
    for d in range(1, chips):
        for b in range(blocks):
            row_copy(d, b).wait_send()

    @pl.when(z == 0)
    def _():
        for d in steps:
            for b in range(blocks):
                for copy in head_sends(d, b):
                    copy.wait_send()

    @pl.when((z > 0) & (z < cols - 1))
    def _():
        for d in steps:
            if forwards(d):
                for b in range(blocks):
                    for side in range(2):
                        left_copy(d, b, left.at[d, b, side], side, side, row, z + 1).wait_send()

    for b in range(blocks):
        out_copy(b).wait()


def shards(channels, weights, slab_in):
    chips, cols = lax.axis_size("row") // 2, lax.axis_size("col")
    _, panels, samples, width = channels.shape
    depth, rows = panels * samples, slab_in.shape[1]
    blocks, tile = 4, 512
    direct = cols <= 4
    high, tiles = rows // blocks, width // tile
    slots = 2 * cols if direct else 3
    others = max(chips - 1, 1)
    dma = pltpu.SemaphoreType.DMA
    hbm = pl.BlockSpec(memory_space=pl.ANY)
    return pl.pallas_call(
        functools.partial(kernel, chips, cols, blocks, direct, tile),
        out_shape=jax.ShapeDtypeStruct(slab_in.shape, F32),
        in_specs=[hbm, pl.BlockSpec(memory_space=pltpu.VMEM), hbm],
        out_specs=hbm,
        scratch_shapes=[
            pltpu.VMEM((2, 2, depth, width), BF16),
            pltpu.VMEM((chips, blocks, 2, 2, high, depth), BF16),
            pltpu.VMEM((chips, 2, blocks, 2, high, depth), BF16),
            pltpu.VMEM((chips, 2, depth, 2 * rows), BF16),
            pltpu.VMEM(weights.shape[::-1], F32),
            pltpu.VMEM(slab_in.shape, F32),
            pltpu.VMEM((others, blocks, 2, high, width), BF16),
            pltpu.VMEM((others, blocks, 2, high, width), BF16),
            dma((tiles,)), dma((tiles,)), dma((tiles,)), dma((chips,)), dma,
            dma((chips, blocks, slots)), dma((chips, blocks, 2)),
            dma((others, blocks)), dma((others, blocks)), dma((blocks,)),
        ],
        compiler_params=pltpu.CompilerParams(
            collective_id=0, has_side_effects=True, vmem_limit_bytes=40 * 2**20),
    )(channels.reshape(2, depth, width), weights, slab_in)


def solution(mesh):
    return jax.shard_map(
        shards,
        mesh=mesh,
        in_specs=(
            P("groups", None, "row", "col"),
            P("groups", None),
            P(None, ("groups", "row"), "col"),
        ),
        out_specs=P(None, ("groups", "row"), "col"),
        check_vma=False,
    )
```

```python
import functools

import jax
import jax.numpy as jnp
from jax import lax
from jax.experimental import pallas as pl
from jax.experimental.pallas import tpu as pltpu
from jax.sharding import PartitionSpec as P

F32, BF16 = jnp.float32, jnp.bfloat16
MESH = pl.DeviceIdType.MESH


def kernel(
    chips, cols, blocks, tile,
    channels, weights, slab, total,
    right, left, split, head, gains, turned, sent, got,
    own_sem, pair_send, pair_recv, head_sem, gain_sem, slab_sem,
    left_send, left_recv, row_send, row_recv,
):
    row, z = lax.axis_index("row"), lax.axis_index("col")
    x, c = row // 2, lax.rem(row, 2)
    pair = row + 1 - 2 * c
    depth, width = channels.shape[1:]
    rows = slab.shape[1]
    high = rows // blocks
    panels = weights.shape[0]
    samples = depth // panels
    tiles = width // tile
    steps = list(range(1, chips)) + [0]

    def peer(d):
        return 2 * lax.rem(x + d, chips) + c

    barrier = pltpu.get_barrier_semaphore()

    def greet(to_row, to_col):
        pl.semaphore_signal(barrier, 1, device_id={"row": to_row, "col": to_col}, device_id_type=MESH)

    greet(pair, z)
    for d in range(1, chips):
        greet(peer(d), z)

    @pl.when(z > 0)
    def _():
        greet(row, z - 1)

    @pl.when(z == 1)
    def _():
        greet(pair, 0)

    def band(b):
        return pl.ds(b * high, high)

    def head_copy(d):
        start = pl.multiple_of(lax.rem(x + d, chips) * (2 * rows), 2 * rows)
        return pltpu.make_async_copy(channels.at[:, :, pl.ds(start, 2 * rows)], head.at[d], head_sem.at[d])

    def own_copy(n):
        span = pl.ds(n * tile, tile)
        return pltpu.make_async_copy(channels.at[:, :, span], right.at[c, :, :, span], own_sem.at[n])

    def pair_copy(n, side):
        span = pl.ds(n * tile, tile)
        return pltpu.make_async_remote_copy(
            channels.at[:, :, span], right.at[side, :, :, span], pair_send.at[n], pair_recv.at[n],
            device_id={"row": pair, "col": z}, device_id_type=MESH)

    def left_copy(d, b, source, side, slot, to_row, to_col):
        return pltpu.make_async_remote_copy(
            source.at[:, band(b)], left.at[d, side, :, band(b)], left_send.at[d, b, slot], left_recv.at[d, b, side],
            device_id={"row": to_row, "col": to_col}, device_id_type=MESH)

    def row_copy(d, b, n):
        span = pl.ds(pl.multiple_of(n * tile, tile), tile)
        return pltpu.make_async_remote_copy(
            sent.at[d - 1, :, band(b), span], got.at[d - 1, :, band(b), span],
            row_send.at[d - 1, b, n], row_recv.at[d - 1, b, n],
            device_id={"row": peer(d), "col": z}, device_id_type=MESH)

    slab_copy = pltpu.make_async_copy(slab, total, slab_sem)
    gain_copy = pltpu.make_async_copy(weights, gains, gain_sem)

    @pl.when(z == 0)
    def _():
        gain_copy.start()
        for d in steps:
            head_copy(d).start()

    for n in range(tiles):
        own_copy(n).start()
    slab_copy.start()

    order = [(d, b) for d in steps for b in range(blocks)]

    def send_next(count):
        for _ in range(count):
            if queue:
                d, b = queue.pop(0)

                @pl.when(z == 0)
                def _():
                    for copy in head_sends(d, b):
                        copy.start()

    def head_sends(d, b):
        copies = []
        if cols > 1:
            copies.append(left_copy(d, b, split.at[d, c], c, 1, row, 1))
            copies.append(left_copy(d, b, split.at[d, 1 - c], c, 2, pair, 1))
        return copies + [left_copy(d, b, split.at[d, 1 - c], c, 0, pair, z)]

    @pl.when(z == 0)
    def _():
        gain_copy.wait()
        scaled = gains[...] / jnp.sum(gains[...])
        turned[...] = scaled.T
        mine = turned[pl.ds(pl.multiple_of(row * samples, samples), samples), :]
        gain = jnp.concatenate([jnp.broadcast_to(mine[:, p:p + 1], (samples, 2 * rows)) for p in range(panels)])
        for d in steps:
            head_copy(d).wait()
            for part in range(2):
                value = (head[d, part].astype(F32) * gain).astype(BF16).T
                for side in range(2):
                    split[d, side, part] = value[side * rows:(side + 1) * rows]
            if d == steps[0]:
                pl.semaphore_wait(barrier, chips + (2 if cols > 1 else 0))
            if d == steps[0]:
                for copy in head_sends(*order[0]):
                    copy.start()
            if d == steps[0]:
                for n in range(tiles):
                    pair_copy(n, c).start()
            left[d, c] = split[d, c]
        for copy in head_sends(*order[0]):
            copy.wait_send()

    @pl.when(z > 0)
    def _():
        pl.semaphore_wait(barrier, 1 + chips - 1 + jnp.where(z < cols - 1, 1, 0))
        for n in range(tiles):
            pair_copy(n, c).start()

    def take_left(d, b):
        @pl.when(z == 0)
        def _():
            left_copy(d, b, left.at[d, 1 - c], 1 - c, 0, pair, z).wait_recv()

        @pl.when(z > 0)
        def _():
            for side in range(2):
                left_copy(d, b, left.at[d, side], side, side, pair, z).wait_recv()

                @pl.when(z < cols - 1)
                def _():
                    left_copy(d, b, left.at[d, side], side, side, row, z + 1).start()

    def multiply(d, low, size, first):
        real, imag = [], []
        for side in range(2):
            re, im = left[d, side, 0, low:low + size], left[d, side, 1, low:low + size]
            real += [re, im]
            imag += [-im, re]
        rows_in = jnp.concatenate([jnp.concatenate(real, axis=1), jnp.concatenate(imag, axis=1)], axis=0)

        def one(n):
            span = pl.ds(pl.multiple_of(n * tile, tile), tile)
            block = right[:, :, :, span].reshape(4 * depth, tile)
            value = jnp.dot(rows_in, block, preferred_element_type=F32).reshape(2, size, tile)
            if d:
                sent[d - 1, :, pl.ds(low, size), span] = value.astype(BF16)
                row_copy(d, low // high, n).start()
            else:
                total[:, pl.ds(low, size), span] += value

        if first:
            for n in range(tiles):
                own_copy(n).wait()
                pair_copy(n, 1 - c).wait_recv()
                one(n)
        else:
            pl.loop(0, tiles)(one)

    queue = order[1:]
    for d in steps[:-1]:
        for b in range(blocks):
            send_next(1 if b < 2 else 2)
            take_left(d, b)
            multiply(d, b * high, high, d == steps[0] and b == 0)
    send_next(len(queue))
    for b in range(blocks):
        take_left(0, b)
    slab_copy.wait()
    multiply(0, 0, rows, chips == 1)

    for b in range(blocks):
        for n in range(tiles):
            span = pl.ds(n * tile, tile)
            for d in range(1, chips):
                row_copy(d, b, n).wait_recv()
                total[:, band(b), span] += got[d - 1, :, band(b), span].astype(F32)

    for n in range(tiles):
        pair_copy(n, c).wait_send()
    for d in range(1, chips):
        for b in range(blocks):
            for n in range(tiles):
                row_copy(d, b, n).wait_send()

    @pl.when(z == 0)
    def _():
        for d, b in order[1:]:
            for copy in head_sends(d, b):
                copy.wait_send()

    @pl.when((z > 0) & (z < cols - 1))
    def _():
        for d in steps:
            for b in range(blocks):
                for side in range(2):
                    left_copy(d, b, left.at[d, side], side, side, row, z + 1).wait_send()

def shards(channels, weights, slab_in):
    chips, cols = lax.axis_size("row") // 2, lax.axis_size("col")
    _, panels, samples, width = channels.shape
    depth, rows = panels * samples, slab_in.shape[1]
    blocks, tile = 4, 512
    tiles = width // tile
    others = max(chips - 1, 1)
    dma = pltpu.SemaphoreType.DMA
    hbm = pl.BlockSpec(memory_space=pltpu.HBM)
    return pl.pallas_call(
        functools.partial(kernel, chips, cols, blocks, tile),
        out_shape=jax.ShapeDtypeStruct(slab_in.shape, F32),
        in_specs=[hbm, hbm, hbm],
        out_specs=pl.BlockSpec(memory_space=pltpu.VMEM),
        scratch_shapes=[
            pltpu.VMEM((2, 2, depth, width), BF16),
            pltpu.VMEM((chips, 2, 2, rows, depth), BF16),
            pltpu.VMEM((chips, 2, 2, rows, depth), BF16),
            pltpu.VMEM((chips, 2, depth, 2 * rows), BF16),
            pltpu.VMEM(weights.shape, F32),
            pltpu.VMEM(weights.shape[::-1], F32),
            pltpu.VMEM((others, 2, rows, width), BF16),
            pltpu.VMEM((others, 2, rows, width), BF16),
            dma((tiles,)), dma((tiles,)), dma((tiles,)), dma((chips,)), dma, dma,
            dma((chips, blocks, 3)), dma((chips, blocks, 2)),
            dma((others, blocks, tiles)), dma((others, blocks, tiles)),
        ],
        compiler_params=pltpu.CompilerParams(
            collective_id=0, has_side_effects=True, vmem_limit_bytes=52 * 2**20),
    )(channels.reshape(2, depth, width), weights, slab_in)


def solution(mesh):
    return jax.shard_map(
        shards,
        mesh=mesh,
        in_specs=(
            P("groups", None, "row", "col"),
            P("groups", None),
            P(None, ("groups", "row"), "col"),
        ),
        out_specs=P(None, ("groups", "row"), "col"),
        check_vma=False,
    )
```

```python
import functools

import jax
import jax.numpy as jnp
from jax import lax
from jax.experimental import pallas as pl
from jax.experimental.pallas import tpu as pltpu
from jax.sharding import PartitionSpec as P

F32, BF16 = jnp.float32, jnp.bfloat16
MESH = pl.DeviceIdType.MESH


def kernel(
    chips, cols, blocks, tile,
    channels, weights, slab, total,
    right, left, split, head, gains, turned, sent, got,
    own_sem, pair_send, pair_recv, head_sem, gain_sem, slab_sem,
    left_send, left_recv, row_send, row_recv,
):
    row, z = lax.axis_index("row"), lax.axis_index("col")
    x, c = row // 2, lax.rem(row, 2)
    pair = row + 1 - 2 * c
    depth, width = channels.shape[1:]
    rows = slab.shape[1]
    high = rows // blocks
    panels = weights.shape[0]
    samples = depth // panels
    tiles = width // tile
    steps = list(range(1, chips)) + [0]

    def peer(d):
        return 2 * lax.rem(x + d, chips) + c

    barrier = pltpu.get_barrier_semaphore()

    def greet(to_row, to_col):
        pl.semaphore_signal(barrier, 1, device_id={"row": to_row, "col": to_col}, device_id_type=MESH)

    greet(pair, z)
    for d in range(1, chips):
        greet(peer(d), z)

    @pl.when(z > 0)
    def _():
        greet(row, z - 1)

    @pl.when(z == 1)
    def _():
        greet(pair, 0)

    def band(b):
        return pl.ds(b * high, high)

    def head_copy(d):
        start = pl.multiple_of(lax.rem(x + d, chips) * (2 * rows), 2 * rows)
        return pltpu.make_async_copy(channels.at[:, :, pl.ds(start, 2 * rows)], head.at[d], head_sem.at[d])

    def own_copy(n):
        span = pl.ds(n * tile, tile)
        return pltpu.make_async_copy(channels.at[:, :, span], right.at[c, :, :, span], own_sem.at[n])

    def pair_copy(n, side):
        span = pl.ds(n * tile, tile)
        return pltpu.make_async_remote_copy(
            channels.at[:, :, span], right.at[side, :, :, span], pair_send.at[n], pair_recv.at[n],
            device_id={"row": pair, "col": z}, device_id_type=MESH)

    def left_copy(d, b, source, side, slot, to_row, to_col):
        return pltpu.make_async_remote_copy(
            source.at[:, band(b)], left.at[d, side, :, band(b)], left_send.at[d, b, slot], left_recv.at[d, b, side],
            device_id={"row": to_row, "col": to_col}, device_id_type=MESH)

    def row_copy(d, b, n):
        span = pl.ds(pl.multiple_of(n * tile, tile), tile)
        return pltpu.make_async_remote_copy(
            sent.at[d - 1, :, band(b), span], got.at[d - 1, :, band(b), span],
            row_send.at[d - 1, b, n], row_recv.at[d - 1, b, n],
            device_id={"row": peer(d), "col": z}, device_id_type=MESH)

    slab_copy = pltpu.make_async_copy(slab, total, slab_sem)
    gain_copy = pltpu.make_async_copy(weights, gains, gain_sem)

    @pl.when(z == 0)
    def _():
        gain_copy.start()
        for d in steps:
            head_copy(d).start()

    for n in range(tiles):
        own_copy(n).start()
    slab_copy.start()

    order = [(d, b) for d in steps for b in range(blocks)]

    def send_next(count):
        for _ in range(count):
            if queue:
                d, b = queue.pop(0)

                @pl.when(z == 0)
                def _():
                    for copy in head_sends(d, b):
                        copy.start()

    def head_sends(d, b):
        copies = []
        if cols > 1:
            copies.append(left_copy(d, b, split.at[d, c], c, 1, row, 1))
            copies.append(left_copy(d, b, split.at[d, 1 - c], c, 2, pair, 1))
        return copies + [left_copy(d, b, split.at[d, 1 - c], c, 0, pair, z)]

    @pl.when(z == 0)
    def _():
        gain_copy.wait()
        scaled = gains[...] / jnp.sum(gains[...])
        turned[...] = scaled.T
        mine = turned[pl.ds(pl.multiple_of(row * samples, samples), samples), :]
        gain = jnp.concatenate([jnp.broadcast_to(mine[:, p:p + 1], (samples, 2 * rows)) for p in range(panels)])
        for d in steps:
            head_copy(d).wait()
            for part in range(2):
                value = (head[d, part].astype(F32) * gain).astype(BF16).T
                for side in range(2):
                    split[d, side, part] = value[side * rows:(side + 1) * rows]
            if d == steps[0]:
                pl.semaphore_wait(barrier, chips + (2 if cols > 1 else 0))
            if d == steps[0]:
                for copy in head_sends(*order[0]):
                    copy.start()
            if d == steps[0]:
                for n in range(tiles):
                    pair_copy(n, c).start()
            left[d, c] = split[d, c]
        for copy in head_sends(*order[0]):
            copy.wait_send()

    @pl.when(z > 0)
    def _():
        pl.semaphore_wait(barrier, 1 + chips - 1 + jnp.where(z < cols - 1, 1, 0))
        for n in range(tiles):
            pair_copy(n, c).start()

    def take_left(d, b):
        @pl.when(z == 0)
        def _():
            left_copy(d, b, left.at[d, 1 - c], 1 - c, 0, pair, z).wait_recv()

        @pl.when(z > 0)
        def _():
            for side in range(2):
                left_copy(d, b, left.at[d, side], side, side, pair, z).wait_recv()

                @pl.when(z < cols - 1)
                def _():
                    left_copy(d, b, left.at[d, side], side, side, row, z + 1).start()

    def multiply(d, low, size, first):
        real, imag = [], []
        for side in range(2):
            re, im = left[d, side, 0, low:low + size], left[d, side, 1, low:low + size]
            real += [re, im]
            imag += [-im, re]
        rows_in = jnp.concatenate([jnp.concatenate(real, axis=1), jnp.concatenate(imag, axis=1)], axis=0)

        def one(n):
            span = pl.ds(pl.multiple_of(n * tile, tile), tile)
            block = right[:, :, :, span].reshape(4 * depth, tile)
            value = jnp.dot(rows_in, block, preferred_element_type=F32).reshape(2, size, tile)
            if d:
                sent[d - 1, :, pl.ds(low, size), span] = value.astype(BF16)
                row_copy(d, low // high, n).start()
            else:
                total[:, pl.ds(low, size), span] += value

        if first:
            for n in range(tiles):
                own_copy(n).wait()
                pair_copy(n, 1 - c).wait_recv()
                one(n)
        else:
            pl.loop(0, tiles)(one)

    queue = order[1:]
    for d in steps[:-1]:
        for b in range(blocks):
            send_next(1 if b < 2 else 2)
            take_left(d, b)
            multiply(d, b * high, high, d == steps[0] and b == 0)
    send_next(len(queue))
    for b in range(blocks):
        take_left(0, b)
    slab_copy.wait()
    multiply(0, 0, rows, chips == 1)

    for b in range(blocks):
        for n in range(tiles):
            span = pl.ds(n * tile, tile)
            for d in range(1, chips):
                row_copy(d, b, n).wait_recv()
                total[:, band(b), span] += got[d - 1, :, band(b), span].astype(F32)

    for n in range(tiles):
        pair_copy(n, c).wait_send()
    for d in range(1, chips):
        for b in range(blocks):
            for n in range(tiles):
                row_copy(d, b, n).wait_send()

    @pl.when(z == 0)
    def _():
        for d, b in order[1:]:
            for copy in head_sends(d, b):
                copy.wait_send()

    @pl.when((z > 0) & (z < cols - 1))
    def _():
        for d in steps:
            for b in range(blocks):
                for side in range(2):
                    left_copy(d, b, left.at[d, side], side, side, row, z + 1).wait_send()

def shards(channels, weights, slab_in):
    chips, cols = lax.axis_size("row") // 2, lax.axis_size("col")
    _, panels, samples, width = channels.shape
    depth, rows = panels * samples, slab_in.shape[1]
    blocks, tile = 4, 512
    tiles = width // tile
    others = max(chips - 1, 1)
    dma = pltpu.SemaphoreType.DMA
    hbm = pl.BlockSpec(memory_space=pltpu.HBM)
    operands = channels.reshape(2, depth, width), weights, slab_in
    return pl.pallas_call(
        functools.partial(kernel, chips, cols, blocks, tile),
        out_shape=jax.ShapeDtypeStruct(slab_in.shape, F32),
        in_specs=[hbm, hbm, hbm],
        out_specs=pl.BlockSpec(memory_space=pltpu.VMEM),
        scratch_shapes=[
            pltpu.VMEM((2, 2, depth, width), BF16),
            pltpu.VMEM((chips, 2, 2, rows, depth), BF16),
            pltpu.VMEM((chips, 2, 2, rows, depth), BF16),
            pltpu.VMEM((chips, 2, depth, 2 * rows), BF16),
            pltpu.VMEM(weights.shape, F32),
            pltpu.VMEM(weights.shape[::-1], F32),
            pltpu.VMEM((others, 2, rows, width), BF16),
            pltpu.VMEM((others, 2, rows, width), BF16),
            dma((tiles,)), dma((tiles,)), dma((tiles,)), dma((chips,)), dma, dma,
            dma((chips, blocks, 3)), dma((chips, blocks, 2)),
            dma((others, blocks, tiles)), dma((others, blocks, tiles)),
        ],
        compiler_params=pltpu.CompilerParams(
            collective_id=0, has_side_effects=True, vmem_limit_bytes=52 * 2**20),
    )(*(pltpu.with_memory_space_constraint(operand, pltpu.HBM) for operand in operands))


def solution(mesh):
    return jax.shard_map(
        shards,
        mesh=mesh,
        in_specs=(
            P("groups", None, "row", "col"),
            P("groups", None),
            P(None, ("groups", "row"), "col"),
        ),
        out_specs=P(None, ("groups", "row"), "col"),
        check_vma=False,
    )
```

```python
import functools

import jax
import jax.numpy as jnp
from jax import lax
from jax.experimental import pallas as pl
from jax.experimental.pallas import tpu as pltpu
from jax.sharding import PartitionSpec as P

F32, BF16 = jnp.float32, jnp.bfloat16
MESH = pl.DeviceIdType.MESH


def kernel(
    chips, cols, blocks, tile,
    channels, weights, slab, total,
    right, left, split, head, gains, turned, sent, got,
    own_sem, pair_send, pair_recv, head_sem, gain_sem, slab_sem,
    left_send, left_recv, row_send, row_recv,
):
    row, z = lax.axis_index("row"), lax.axis_index("col")
    x, c = row // 2, lax.rem(row, 2)
    pair = row + 1 - 2 * c
    depth, width = channels.shape[1:]
    rows = slab.shape[1]
    high = rows // blocks
    panels = weights.shape[0]
    samples = depth // panels
    tiles = width // tile
    steps = list(range(1, chips)) + [0]

    def peer(d):
        return 2 * lax.rem(x + d, chips) + c

    barrier = pltpu.get_barrier_semaphore()

    def greet(to_row, to_col):
        pl.semaphore_signal(barrier, 1, device_id={"row": to_row, "col": to_col}, device_id_type=MESH)

    greet(pair, z)
    for d in range(1, chips):
        greet(peer(d), z)

    @pl.when(z > 0)
    def _():
        greet(row, z - 1)

    @pl.when(z == 1)
    def _():
        greet(pair, 0)

    def band(b):
        return pl.ds(b * high, high)

    def head_copy(d):
        start = pl.multiple_of(lax.rem(x + d, chips) * (2 * rows), 2 * rows)
        return pltpu.make_async_copy(channels.at[:, :, pl.ds(start, 2 * rows)], head.at[d], head_sem.at[d])

    def own_copy(n):
        span = pl.ds(n * tile, tile)
        return pltpu.make_async_copy(channels.at[:, :, span], right.at[c, :, :, span], own_sem.at[n])

    def pair_copy(n, side):
        span = pl.ds(n * tile, tile)
        return pltpu.make_async_remote_copy(
            channels.at[:, :, span], right.at[side, :, :, span], pair_send.at[n], pair_recv.at[n],
            device_id={"row": pair, "col": z}, device_id_type=MESH)

    def left_copy(d, b, source, side, slot, to_row, to_col):
        return pltpu.make_async_remote_copy(
            source.at[:, band(b)], left.at[d, side, :, band(b)], left_send.at[d, b, slot], left_recv.at[d, b, side],
            device_id={"row": to_row, "col": to_col}, device_id_type=MESH)

    def row_copy(d, b, n):
        span = pl.ds(pl.multiple_of(n * tile, tile), tile)
        return pltpu.make_async_remote_copy(
            sent.at[d - 1, :, band(b), span], got.at[d - 1, :, band(b), span],
            row_send.at[d - 1, b, n], row_recv.at[d - 1, b, n],
            device_id={"row": peer(d), "col": z}, device_id_type=MESH)

    slab_copy = pltpu.make_async_copy(slab, total, slab_sem)
    gain_copy = pltpu.make_async_copy(weights, gains, gain_sem)

    @pl.when(z == 0)
    def _():
        gain_copy.start()
        for d in steps:
            head_copy(d).start()

    for n in range(tiles):
        own_copy(n).start()
    slab_copy.start()

    order = [(d, b) for d in steps for b in range(blocks)]

    def send_next(count):
        for _ in range(count):
            if queue:
                d, b = queue.pop(0)

                @pl.when(z == 0)
                def _():
                    for copy in head_sends(d, b):
                        copy.start()

    def head_sends(d, b):
        copies = []
        if cols > 1:
            copies.append(left_copy(d, b, split.at[d, c], c, 1, row, 1))
            copies.append(left_copy(d, b, split.at[d, 1 - c], c, 2, pair, 1))
        return copies + [left_copy(d, b, split.at[d, 1 - c], c, 0, pair, z)]

    @pl.when(z == 0)
    def _():
        gain_copy.wait()
        scaled = gains[...] / jnp.sum(gains[...])
        turned[...] = scaled.T
        mine = turned[pl.ds(pl.multiple_of(row * samples, samples), samples), :]
        gain = jnp.concatenate([jnp.broadcast_to(mine[:, p:p + 1], (samples, 2 * rows)) for p in range(panels)])
        for d in steps:
            head_copy(d).wait()
            for part in range(2):
                value = (head[d, part].astype(F32) * gain).astype(BF16).T
                for side in range(2):
                    split[d, side, part] = value[side * rows:(side + 1) * rows]
            if d == steps[0]:
                pl.semaphore_wait(barrier, chips + (2 if cols > 1 else 0))
            if d == steps[0]:
                for copy in head_sends(*order[0]):
                    copy.start()
            if d == steps[0]:
                for n in range(tiles):
                    pair_copy(n, c).start()
            left[d, c] = split[d, c]
        for copy in head_sends(*order[0]):
            copy.wait_send()

    @pl.when(z > 0)
    def _():
        pl.semaphore_wait(barrier, 1 + chips - 1 + jnp.where(z < cols - 1, 1, 0))
        for n in range(tiles):
            pair_copy(n, c).start()

    def take_left(d, b):
        @pl.when(z == 0)
        def _():
            left_copy(d, b, left.at[d, 1 - c], 1 - c, 0, pair, z).wait_recv()

        @pl.when(z > 0)
        def _():
            for side in range(2):
                left_copy(d, b, left.at[d, side], side, side, pair, z).wait_recv()

                @pl.when(z < cols - 1)
                def _():
                    left_copy(d, b, left.at[d, side], side, side, row, z + 1).start()

    def multiply(d, low, size, first):
        real, imag = [], []
        for side in range(2):
            re, im = left[d, side, 0, low:low + size], left[d, side, 1, low:low + size]
            real += [re, im]
            imag += [-im, re]
        rows_in = jnp.concatenate([jnp.concatenate(real, axis=1), jnp.concatenate(imag, axis=1)], axis=0)

        def one(n):
            span = pl.ds(pl.multiple_of(n * tile, tile), tile)
            block = right[:, :, :, span].reshape(4 * depth, tile)
            value = jnp.dot(rows_in, block, preferred_element_type=F32).reshape(2, size, tile)
            if d:
                sent[d - 1, :, pl.ds(low, size), span] = value.astype(BF16)
                row_copy(d, low // high, n).start()
            else:
                total[:, pl.ds(low, size), span] += value

        if first:
            for n in range(tiles):
                own_copy(n).wait()
                pair_copy(n, 1 - c).wait_recv()
                one(n)
        else:
            pl.loop(0, tiles)(one)

    queue = order[1:]
    for d in steps[:-1]:
        for b in range(blocks):
            send_next(2)
            take_left(d, b)
            multiply(d, b * high, high, d == steps[0] and b == 0)
    send_next(len(queue))
    for b in range(blocks):
        take_left(0, b)
    slab_copy.wait()
    multiply(0, 0, rows, chips == 1)

    for b in range(blocks):
        for n in range(tiles):
            span = pl.ds(n * tile, tile)
            for d in range(1, chips):
                row_copy(d, b, n).wait_recv()
                total[:, band(b), span] += got[d - 1, :, band(b), span].astype(F32)

    for n in range(tiles):
        pair_copy(n, c).wait_send()
    for d in range(1, chips):
        for b in range(blocks):
            for n in range(tiles):
                row_copy(d, b, n).wait_send()

    @pl.when(z == 0)
    def _():
        for d, b in order[1:]:
            for copy in head_sends(d, b):
                copy.wait_send()

    @pl.when((z > 0) & (z < cols - 1))
    def _():
        for d in steps:
            for b in range(blocks):
                for side in range(2):
                    left_copy(d, b, left.at[d, side], side, side, row, z + 1).wait_send()

def shards(channels, weights, slab_in):
    chips, cols = lax.axis_size("row") // 2, lax.axis_size("col")
    _, panels, samples, width = channels.shape
    depth, rows = panels * samples, slab_in.shape[1]
    blocks, tile = 4, 512
    tiles = width // tile
    others = max(chips - 1, 1)
    dma = pltpu.SemaphoreType.DMA
    hbm = pl.BlockSpec(memory_space=pltpu.HBM)
    operands = channels.reshape(2, depth, width), weights, slab_in
    return pl.pallas_call(
        functools.partial(kernel, chips, cols, blocks, tile),
        out_shape=jax.ShapeDtypeStruct(slab_in.shape, F32),
        in_specs=[hbm, hbm, hbm],
        out_specs=pl.BlockSpec(memory_space=pltpu.VMEM),
        scratch_shapes=[
            pltpu.VMEM((2, 2, depth, width), BF16),
            pltpu.VMEM((chips, 2, 2, rows, depth), BF16),
            pltpu.VMEM((chips, 2, 2, rows, depth), BF16),
            pltpu.VMEM((chips, 2, depth, 2 * rows), BF16),
            pltpu.VMEM(weights.shape, F32),
            pltpu.VMEM(weights.shape[::-1], F32),
            pltpu.VMEM((others, 2, rows, width), BF16),
            pltpu.VMEM((others, 2, rows, width), BF16),
            dma((tiles,)), dma((tiles,)), dma((tiles,)), dma((chips,)), dma, dma,
            dma((chips, blocks, 3)), dma((chips, blocks, 2)),
            dma((others, blocks, tiles)), dma((others, blocks, tiles)),
        ],
        compiler_params=pltpu.CompilerParams(
            collective_id=0, has_side_effects=True, vmem_limit_bytes=52 * 2**20),
    )(*(pltpu.with_memory_space_constraint(operand, pltpu.HBM) for operand in operands))


def solution(mesh):
    return jax.shard_map(
        shards,
        mesh=mesh,
        in_specs=(
            P("groups", None, "row", "col"),
            P("groups", None),
            P(None, ("groups", "row"), "col"),
        ),
        out_specs=P(None, ("groups", "row"), "col"),
        check_vma=False,
    )
```

```python
import functools

import jax
import jax.numpy as jnp
from jax import lax
from jax.experimental import pallas as pl
from jax.experimental.pallas import tpu as pltpu
from jax.sharding import PartitionSpec as P

F32, BF16 = jnp.float32, jnp.bfloat16
MESH = pl.DeviceIdType.MESH


def kernel(
    chips, cols, blocks, tile,
    channels, weights, slab, total,
    right, left, split, head, gains, turned, sent, got,
    own_sem, pair_send, pair_recv, head_sem, gain_sem, slab_sem,
    left_send, left_recv, row_send, row_recv,
):
    row, z = lax.axis_index("row"), lax.axis_index("col")
    x, c = row // 2, lax.rem(row, 2)
    pair = row + 1 - 2 * c
    depth, width = channels.shape[1:]
    rows = slab.shape[1]
    high = rows // blocks
    panels = weights.shape[0]
    samples = depth // panels
    tiles = width // tile
    steps = list(range(1, chips)) + [0]

    def peer(d):
        return 2 * lax.rem(x + d, chips) + c

    barrier = pltpu.get_barrier_semaphore()

    def greet(to_row, to_col):
        pl.semaphore_signal(barrier, 1, device_id={"row": to_row, "col": to_col}, device_id_type=MESH)

    greet(pair, z)
    for d in range(1, chips):
        greet(peer(d), z)

    @pl.when(z > 0)
    def _():
        greet(row, z - 1)

    @pl.when(z == 1)
    def _():
        greet(pair, 0)

    def band(b):
        return pl.ds(b * high, high)

    def head_copy(d):
        start = pl.multiple_of(lax.rem(x + d, chips) * (2 * rows), 2 * rows)
        return pltpu.make_async_copy(channels.at[:, :, pl.ds(start, 2 * rows)], head.at[d], head_sem.at[d])

    def own_copy(n):
        span = pl.ds(n * tile, tile)
        return pltpu.make_async_copy(channels.at[:, :, span], right.at[c, :, :, span], own_sem.at[n])

    def pair_copy(n, side):
        span = pl.ds(n * tile, tile)
        return pltpu.make_async_remote_copy(
            channels.at[:, :, span], right.at[side, :, :, span], pair_send.at[n], pair_recv.at[n],
            device_id={"row": pair, "col": z}, device_id_type=MESH)

    def left_copy(d, b, source, side, slot, to_row, to_col):
        return pltpu.make_async_remote_copy(
            source.at[:, band(b)], left.at[d, side, :, band(b)], left_send.at[d, b, slot], left_recv.at[d, b, side],
            device_id={"row": to_row, "col": to_col}, device_id_type=MESH)

    def row_copy(d, b, n):
        span = pl.ds(pl.multiple_of(n * tile, tile), tile)
        return pltpu.make_async_remote_copy(
            sent.at[d - 1, :, band(b), span], got.at[d - 1, :, band(b), span],
            row_send.at[d - 1, b, n], row_recv.at[d - 1, b, n],
            device_id={"row": peer(d), "col": z}, device_id_type=MESH)

    slab_copy = pltpu.make_async_copy(slab, total, slab_sem)
    gain_copy = pltpu.make_async_copy(weights, gains, gain_sem)

    @pl.when(z == 0)
    def _():
        gain_copy.start()
        for d in steps:
            head_copy(d).start()

    for n in range(tiles):
        own_copy(n).start()
    slab_copy.start()

    order = [(d, b) for d in steps for b in range(blocks)]

    def send_next(count):
        for _ in range(count):
            if queue:
                d, b = queue.pop(0)

                @pl.when(z == 0)
                def _():
                    for copy in head_sends(d, b):
                        copy.start()

    def head_sends(d, b):
        copies = []
        if cols > 1:
            copies.append(left_copy(d, b, split.at[d, c], c, 1, row, 1))
            copies.append(left_copy(d, b, split.at[d, 1 - c], c, 2, pair, 1))
        return copies + [left_copy(d, b, split.at[d, 1 - c], c, 0, pair, z)]

    @pl.when(z == 0)
    def _():
        gain_copy.wait()
        scaled = gains[...] / jnp.sum(gains[...])
        turned[...] = scaled.T
        mine = turned[pl.ds(pl.multiple_of(row * samples, samples), samples), :]
        gain = jnp.concatenate([jnp.broadcast_to(mine[:, p:p + 1], (samples, 2 * rows)) for p in range(panels)])
        for d in steps:
            head_copy(d).wait()
            for part in range(2):
                value = (head[d, part].astype(F32) * gain).astype(BF16).T
                for side in range(2):
                    split[d, side, part] = value[side * rows:(side + 1) * rows]
            if d == steps[0]:
                pl.semaphore_wait(barrier, chips + (2 if cols > 1 else 0))
            if d == steps[0]:
                for copy in head_sends(*order[0]):
                    copy.start()
            if d == steps[0]:
                for n in range(tiles):
                    pair_copy(n, c).start()
            left[d, c] = split[d, c]
        for copy in head_sends(*order[0]):
            copy.wait_send()

    @pl.when(z > 0)
    def _():
        pl.semaphore_wait(barrier, 1 + chips - 1 + jnp.where(z < cols - 1, 1, 0))
        for n in range(tiles):
            pair_copy(n, c).start()

    def take_left(d, b):
        @pl.when(z == 0)
        def _():
            left_copy(d, b, left.at[d, 1 - c], 1 - c, 0, pair, z).wait_recv()

        @pl.when(z > 0)
        def _():
            for side in range(2):
                left_copy(d, b, left.at[d, side], side, side, pair, z).wait_recv()

                @pl.when(z < cols - 1)
                def _():
                    left_copy(d, b, left.at[d, side], side, side, row, z + 1).start()

    def multiply(d, low, size, first):
        real, imag = [], []
        for side in range(2):
            re, im = left[d, side, 0, low:low + size], left[d, side, 1, low:low + size]
            real += [re, im]
            imag += [-im, re]
        rows_in = jnp.concatenate([jnp.concatenate(real, axis=1), jnp.concatenate(imag, axis=1)], axis=0)

        def one(n):
            span = pl.ds(pl.multiple_of(n * tile, tile), tile)
            block = right[:, :, :, span].reshape(4 * depth, tile)
            value = jnp.dot(rows_in, block, preferred_element_type=F32).reshape(2, size, tile)
            if d:
                sent[d - 1, :, pl.ds(low, size), span] = value.astype(BF16)
                row_copy(d, low // high, n).start()
            else:
                total[:, pl.ds(low, size), span] += value

        if first:
            for n in range(tiles):
                own_copy(n).wait()
                pair_copy(n, 1 - c).wait_recv()
                one(n)
        else:
            pl.loop(0, tiles)(one)

    queue = order[1:]
    for d in steps[:-1]:
        for b in range(blocks):
            send_next(2)
            take_left(d, b)
            multiply(d, b * high, high, d == steps[0] and b == 0)
    send_next(len(queue))
    for b in range(blocks):
        take_left(0, b)
    slab_copy.wait()
    multiply(0, 0, rows, chips == 1)

    for b in range(blocks):
        for n in range(tiles):
            span = pl.ds(n * tile, tile)
            for d in range(1, chips):
                row_copy(d, b, n).wait_recv()
                total[:, band(b), span] += got[d - 1, :, band(b), span].astype(F32)

    for n in range(tiles):
        pair_copy(n, c).wait_send()
    for d in range(1, chips):
        for b in range(blocks):
            for n in range(tiles):
                row_copy(d, b, n).wait_send()

    @pl.when(z == 0)
    def _():
        for d, b in order[1:]:
            for copy in head_sends(d, b):
                copy.wait_send()

    @pl.when((z > 0) & (z < cols - 1))
    def _():
        for d in steps:
            for b in range(blocks):
                for side in range(2):
                    left_copy(d, b, left.at[d, side], side, side, row, z + 1).wait_send()

def shards(channels, weights, slab_in):
    chips, cols = lax.axis_size("row") // 2, lax.axis_size("col")
    _, panels, samples, width = channels.shape
    depth, rows = panels * samples, slab_in.shape[1]
    blocks, tile = 4, 1024
    tiles = width // tile
    others = max(chips - 1, 1)
    dma = pltpu.SemaphoreType.DMA
    hbm = pl.BlockSpec(memory_space=pltpu.HBM)
    operands = channels.reshape(2, depth, width), weights, slab_in
    return pl.pallas_call(
        functools.partial(kernel, chips, cols, blocks, tile),
        out_shape=jax.ShapeDtypeStruct(slab_in.shape, F32),
        in_specs=[hbm, hbm, hbm],
        out_specs=pl.BlockSpec(memory_space=pltpu.VMEM),
        scratch_shapes=[
            pltpu.VMEM((2, 2, depth, width), BF16),
            pltpu.VMEM((chips, 2, 2, rows, depth), BF16),
            pltpu.VMEM((chips, 2, 2, rows, depth), BF16),
            pltpu.VMEM((chips, 2, depth, 2 * rows), BF16),
            pltpu.VMEM(weights.shape, F32),
            pltpu.VMEM(weights.shape[::-1], F32),
            pltpu.VMEM((others, 2, rows, width), BF16),
            pltpu.VMEM((others, 2, rows, width), BF16),
            dma((tiles,)), dma((tiles,)), dma((tiles,)), dma((chips,)), dma, dma,
            dma((chips, blocks, 3)), dma((chips, blocks, 2)),
            dma((others, blocks, tiles)), dma((others, blocks, tiles)),
        ],
        compiler_params=pltpu.CompilerParams(
            collective_id=0, has_side_effects=True, vmem_limit_bytes=52 * 2**20),
    )(*(pltpu.with_memory_space_constraint(operand, pltpu.HBM) for operand in operands))


def solution(mesh):
    return jax.shard_map(
        shards,
        mesh=mesh,
        in_specs=(
            P("groups", None, "row", "col"),
            P("groups", None),
            P(None, ("groups", "row"), "col"),
        ),
        out_specs=P(None, ("groups", "row"), "col"),
        check_vma=False,
    )
```
